256 devices in a mesh: dp: 8 (over z_hi, x), expert: 32 (over y, z_lo, core).
Axes of the slice: x: 4, y: 4, z: 8 (z_hi: 2, z_lo: 4; z = z_hi * 4 + z_lo), core: 2. Of those that a mesh axis runs over, the one named last changes fastest.
Arguments:
- tokens_x: bfloat16 [4096, 4096], P('expert'), may hold values from -6 to 6
- cotangent: bfloat16 [4096, 4096], P('expert'), may hold values from -1.5 to 1.5
- expert_ids: int32 [4096, 2], P('expert'), may hold values from 0 to 31, all different within a row; in each aligned block of 128 rows (0 to 127, 128 to 255, ...) at most 16 rows name the same one
- gate_weights: float32 [4096, 2], P('expert'), may hold values from 0.1 to 1
- w_gate: bfloat16 [32, 1536, 4096], P('expert', 'dp'), may hold values from -0.09375 to 0.09375
- w_up: bfloat16 [32, 1536, 4096], P('expert', 'dp'), may hold values from -0.09375 to 0.09375
- w_down: bfloat16 [32, 1536, 4096], P('expert', 'dp'), may hold values from -0.15625 to 0.15625
Outputs:
- grad_tokens: bfloat16 [4096, 4096], P('expert', 'dp')
- grad_gate: bfloat16 [32, 1536, 4096], P('expert', 'dp')
- grad_up: bfloat16 [32, 1536, 4096], P('expert', 'dp')
- grad_down: bfloat16 [32, 1536, 4096], P('expert', 'dp')
The draws below stay inside these ranges and needn't reach their ends.
Inputs may be any that keep to these rules, and one draw needn't show every extreme that they name: `expert_ids`: within the rows of one device (aligned blocks of 128 tokens) no expert is named by more than 16 routes, a bound that some block reaches; the routes of a token name different experts.
All inputs are finite; a program needn't handle non-finite values.
Results may differ from the reference program's by a relative error of at most 0.017.
Values may be sent and summed in bfloat16 or wider, within the bound.
A program may use at most 128 MiB of HBM per device.

```python
import math
import jax
import jax.numpy as jnp
import numpy as np
from jax import lax

D = 4096
FF = 1536
TOK_ROWS = 128
ROUTES = 2
EXPERTS = 32
TOKENS = 4096
CAP = 16
FF_DEV = 192
N_EXPERT = 32


def block_levels(key, extent, split, smallest, high):
    gain, own = 1.0, jax.random.fold_in(key, 6)
    for dim, blocks in split:
        heights = jnp.exp(jax.random.uniform(jax.random.fold_in(own, dim), (blocks,), jnp.float32, smallest / len(split), high / len(split)))
        gain = gain * jnp.repeat(heights, extent[dim] // blocks).reshape([-1 if axis == dim else 1 for axis in range(len(extent))])
    return gain


def deal_out(key, own, number, rows, amount, top, most, skew):
    order = jax.random.permutation(key, amount)
    crowded, usual = load_shares(amount, rows * top, most, skew, True), load_shares(amount, rows * top, most, skew, False)
    places = jnp.arange(amount)

    def named(sizes, rotation):
        used = int((sizes > 0).sum())
        fixed = max(1, used // 4)
        moved = fixed + (places - fixed + rotation * (used - fixed)) % max(1, amount - fixed)
        return jnp.zeros((amount,), jnp.int32).at[order[jnp.where(places < fixed, places, moved)]].set(jnp.asarray(sizes, jnp.int32))

    sizes = jnp.where(number % 4 == 0, named(crowded, number // 4), named(usual, number - number // 4 - 1))
    mixed = jax.random.permutation(jax.random.fold_in(own, 3), amount)
    giver, sink = mixed[0:amount // 2 * 2:2], mixed[1:amount // 2 * 2:2]
    margin = jnp.minimum(sizes[giver] - 1, most - sizes[sink]) // 2
    margin = jnp.where((giver == order[0]) | (sink == order[0]) | (sizes[sink] == 0), 0, jnp.maximum(margin, 0))
    moved = jax.random.randint(jax.random.fold_in(own, 4), (amount // 2,), 0, 1 << 20) % (margin + 1)
    sizes = sizes.at[giver].add(-moved).at[sink].add(moved)
    members = jnp.searchsorted(jnp.cumsum(sizes), jnp.arange(rows * top), side="right").astype(jnp.int32)
    listing = members.reshape(top, rows).T
    listing = listing[jax.random.permutation(jax.random.fold_in(own, 1), rows)]
    rotation = jax.random.randint(jax.random.fold_in(own, 2), (rows, 1), 0, top)
    return jnp.take_along_axis(listing, (jnp.arange(top)[None, :] + rotation) % top, axis=1)


def load_shares(amount, total, reach, slope, full):
    weights = [(1 << 20) // math.isqrt(grade ** slope) + 1 for grade in range(1, amount + 1)]
    largest = reach if full else min(reach, max(-(-total // amount), total * weights[0] // sum(weights)))
    least = 1 if total - largest >= amount - 1 else 0
    given, rest = [largest] + [least] * (amount - 1), total - largest - least * (amount - 1)
    while rest > 0:
        free = [i for i in range(1, amount) if given[i] < largest] or [i for i in range(1, amount) if given[i] < reach]
        pool, remaining = sum([weights[i] for i in free]), rest
        for i in free:
            extra = min(reach - given[i], max(1, remaining * weights[i] // pool), rest)
            given[i] = given[i] + extra
            rest = rest - extra
    return np.array(given)


def noise(stream_key, dims, width, bound, cuts=(), kind=jnp.bfloat16):
    values = jax.random.normal(stream_key, dims, jnp.float32) * width
    if len(cuts) > 0:
        values = block_levels(stream_key, dims, cuts, -0.22, 0.18) * values
    return jnp.clip(values, min=-bound, max=bound).astype(kind)


def setup_inputs(seed: int = 0) -> dict:
    key_list = jax.random.split(jax.random.key(seed), 8)
    tokens_x = noise(key_list[0], (TOKENS, D), 1.0, 6.0, ((0, 32),))
    cotangent = noise(key_list[1], (TOKENS, D), 0.25, 1.5, ((0, 32),))
    expert_ids_keys = jax.random.split(jax.random.fold_in(key_list[2], 1), TOKENS // TOK_ROWS)
    expert_ids_turns = jax.random.permutation(jax.random.fold_in(key_list[2], 3), TOKENS // TOK_ROWS)
    expert_ids = jax.vmap(lambda own, number: deal_out(jax.random.fold_in(key_list[2], 2), own, number, TOK_ROWS, EXPERTS, ROUTES, CAP, 2))(expert_ids_keys, expert_ids_turns).reshape((TOKENS, ROUTES))
    gate_weights = jnp.clip(0.1 + 0.9 * jax.random.uniform(key_list[3], (TOKENS, ROUTES), jnp.float32) ** block_levels(key_list[3], (TOKENS, ROUTES), ((0, 32),), -0.2, 0.2), 0.1, 1.0)
    w_gate = noise(key_list[4], (EXPERTS, FF, D), D ** -0.5, 0.09375, ((0, 32), (1, 8)))
    w_up = noise(key_list[5], (EXPERTS, FF, D), D ** -0.5, 0.09375, ((0, 32), (1, 8)))
    w_down = noise(key_list[6], (EXPERTS, FF, D), FF ** -0.5, 0.15625, ((0, 32), (1, 8)))
    return dict(tokens_x=tokens_x, cotangent=cotangent, expert_ids=expert_ids, gate_weights=gate_weights, w_gate=w_gate, w_up=w_up, w_down=w_down)


def round_keep(values):
    return lax.optimization_barrier(values.astype(jnp.bfloat16)).astype(jnp.float32)


def reference(tokens_x, cotangent, expert_ids, gate_weights, w_gate, w_up, w_down):
    route_total = TOKENS * ROUTES
    most_rows = N_EXPERT * CAP
    flat_ids = expert_ids.reshape(-1).astype(jnp.int32)
    route_order = jnp.argsort(flat_ids, stable=True).astype(jnp.int32)
    counts = jnp.sum((flat_ids[:, None] == jnp.arange(EXPERTS, dtype=jnp.int32)[None, :]).astype(jnp.int32), axis=0).astype(jnp.int32)
    starts = (jnp.cumsum(counts) - counts).astype(jnp.int32)
    padded_order = jnp.concatenate([route_order, jnp.zeros((most_rows,), jnp.int32)])
    route_token = jnp.arange(route_total, dtype=jnp.int32) // ROUTES
    scaled_all = (gate_weights.reshape(-1)[:, None] * cotangent[route_token].astype(jnp.float32)).astype(jnp.bfloat16)

    def one_expert(expert_index):
        slot_rows = lax.dynamic_slice(padded_order, (starts[expert_index],), (most_rows,)).astype(jnp.int32)
        valid_rows = jnp.arange(most_rows, dtype=jnp.int32) < counts[expert_index]
        target = jnp.where(valid_rows, slot_rows, route_total).astype(jnp.int32)
        inputs = jnp.where(valid_rows[:, None], tokens_x[slot_rows // ROUTES].astype(jnp.float32), 0.0)
        scaled = jnp.where(valid_rows[:, None], scaled_all[slot_rows].astype(jnp.float32), 0.0)
        weight_gate = w_gate[expert_index].astype(jnp.float32)
        weight_up = w_up[expert_index].astype(jnp.float32)
        weight_down = w_down[expert_index].astype(jnp.float32)
        gate_pre = jnp.dot(inputs, weight_gate.T)
        up_pre = jnp.dot(inputs, weight_up.T)
        sigmoid = jax.nn.sigmoid(gate_pre)
        swish_value = gate_pre * sigmoid
        activation = round_keep(swish_value * up_pre)
        act_grad = jnp.dot(scaled, weight_down.T)
        slope_term = sigmoid * (1.0 + gate_pre * (1.0 - sigmoid))
        gate_grad = round_keep(act_grad * up_pre * slope_term)
        up_grad = round_keep(act_grad * swish_value)
        grad_down = jnp.dot(activation.T, scaled).astype(jnp.bfloat16)
        grad_gate = jnp.dot(gate_grad.T, inputs).astype(jnp.bfloat16)
        grad_up = jnp.dot(up_grad.T, inputs).astype(jnp.bfloat16)
        blocks = FF // FF_DEV
        gate_blocks = gate_grad.reshape(most_rows, blocks, FF_DEV)
        up_blocks = up_grad.reshape(most_rows, blocks, FF_DEV)
        wg_blocks = weight_gate.reshape(blocks, FF_DEV, D)
        wu_blocks = weight_up.reshape(blocks, FF_DEV, D)
        block_part = jnp.einsum("mjf,jfd->mjd", gate_blocks, wg_blocks) + jnp.einsum("mjf,jfd->mjd", up_blocks, wu_blocks)
        route_rows = jnp.sum(round_keep(block_part), axis=1)
        return grad_gate, grad_up, grad_down, route_rows, target

    grad_gate, grad_up, grad_down, route_rows, target = lax.map(one_expert, jnp.arange(EXPERTS, dtype=jnp.int32))
    routed = jnp.zeros((route_total + 1, D), jnp.float32).at[target.reshape(-1)].add(route_rows.reshape(-1, D))
    grad_tokens = jnp.sum(routed[:route_total].reshape(TOKENS, ROUTES, D), axis=1).astype(jnp.bfloat16)
    return grad_tokens, grad_gate, grad_up, grad_down
```

```python
import functools

import jax
import jax.numpy as jnp
from jax import lax
from jax.experimental import pallas as pl
from jax.experimental.pallas import tpu as pltpu
from jax.sharding import PartitionSpec as P

MESH = pl.DeviceIdType.MESH
F32, BF16 = jnp.float32, jnp.bfloat16
D = 4096
HALF = 2048
QUARTER = 1024
BLOCK = 512
FF = 192
TOK = 128
CAP = 16
EXPERTS = 32
ROWS = EXPERTS * CAP
CHUNKS = 4
PER = EXPERTS // CHUNKS
CROWS = ROWS // CHUNKS

Z_C = ((1, 0), (-1, 0), (2, 0), (0, 1), (-1, 1), (1, 1), (-2, 1), (0, 0))
MESSAGES = tuple(
    (dy,) + Z_C[(k + 2 * n) % 8] for k in range(8) for n, dy in enumerate((1, 3, 2, 0))
)
SELF = MESSAGES.index((0, 0, 0))
REMOTE = tuple(i for i in range(EXPERTS) if i != SELF)


def nt(left, right):
    return lax.dot_general(left, right, (((1,), (1,)), ((), ())), preferred_element_type=F32)


def nn(left, right):
    return lax.dot_general(left, right, (((1,), (0,)), ((), ())), preferred_element_type=F32)


def tn(left, right):
    return lax.dot_general(left, right, (((0,), (0,)), ((), ())), preferred_element_type=F32)


def kernel(
    route_ref, tok_hbm, cot_hbm, wg_hbm, wu_hbm, wd_hbm,
    gt_ref, gg_hbm, gu_hbm, gd_hbm,
    tok, weights, onehot, gates, sent, arrived, act, ggrad, ugrad,
    part_own, part_out, part_in, summed, returned, combined, fin_out, fin_in, grads,
    tok_sem, w_sem, self_sem, a_send, a_recv, x_send, x_recv, p_send, p_recv, r_send, r_recv, f_send, f_recv, g_sem,
):
    dp, ex = lax.axis_index("dp"), lax.axis_index("expert")
    h, x = dp // 4, dp % 4
    y, l, c = ex // 8, (ex // 2) % 4, ex % 2
    z = h * 4 + l
    p = x % 2
    q = 1 - p

    def at(dx, dy, dz, dc):
        zz = (z + dz + 8) % 8
        return (
            (zz // 4) * 4 + (x + dx + 4) % 4,
            ((y + dy + 4) % 4) * 8 + (zz % 4) * 2 + (c + dc) % 2,
        )

    ins = []
    for i, src in enumerate((tok_hbm, cot_hbm)):
        for j in range(4):
            cols = pl.ds(pl.multiple_of((2 * j + p) * BLOCK, BLOCK), BLOCK)
            ins.append(
                pltpu.make_async_copy(
                    src.at[:, cols], tok.at[i, :, pl.ds(j * BLOCK, BLOCK)], tok_sem.at[4 * i + j]
                )
            )
    w_ins = []
    for i, src in enumerate((wg_hbm, wu_hbm, wd_hbm)):
        for b in range(8):
            w_ins.append(
                pltpu.make_async_copy(
                    src.at[:, pl.ds(b * BLOCK, BLOCK)],
                    weights.at[i, b % 2, :, pl.ds((b // 2) * BLOCK, BLOCK)],
                    w_sem.at[8 * i + b],
                )
            )
    for copy in ins:
        copy.start()
    for copy in w_ins:
        copy.start()

    barrier = pltpu.get_barrier_semaphore()
    peers = [(0,) + MESSAGES[i] for i in REMOTE]
    peers += [(0, dy, -dz, dc) for dy, dz, dc in MESSAGES if abs(dz) == 2]
    peers += [(1, 0, 0, 0), (-1, 0, 0, 0), (2, 0, 0, 0), (0, 0, 4, 0), (2, 0, 4, 0)]
    for peer in peers:
        pl.semaphore_signal(barrier, inc=1, device_id=at(*peer), device_id_type=MESH)

    ids0, ids1 = route_ref[0:1, :], route_ref[1:2, :]
    gate0, gate1 = route_ref[2:3, :], route_ref[3:4, :]
    expert_row = lax.broadcasted_iota(jnp.int32, (EXPERTS, TOK), 0).astype(F32)
    earlier = (
        lax.broadcasted_iota(jnp.int32, (TOK, TOK), 0)
        < lax.broadcasted_iota(jnp.int32, (TOK, TOK), 1)
    )
    earlier = jnp.where(earlier, 1.0, 0.0).astype(BF16)
    hot0 = jnp.where(expert_row == ids0, 1.0, 0.0)
    hot1 = jnp.where(expert_row == ids1, 1.0, 0.0)
    before0 = nn(hot0.astype(BF16), earlier)
    before1 = nn(hot1.astype(BF16), earlier) + jnp.sum(hot0, axis=1, keepdims=True)
    rank0 = jnp.sum(hot0 * before0, axis=0, keepdims=True)
    rank1 = jnp.sum(hot1 * before1, axis=0, keepdims=True)
    slot_row = lax.broadcasted_iota(jnp.int32, (CAP, TOK), 0).astype(F32)
    for i, (dy, dz, dc) in enumerate(MESSAGES):
        expert = (((y + dy) % 4) * 8 + ((l + dz + 4) % 4) * 2 + (c + dc) % 2).astype(F32)
        is0 = (slot_row == rank0) & (ids0 == expert)
        is1 = (slot_row == rank1) & (ids1 == expert)
        rows = pl.ds(i * CAP, CAP)
        onehot[rows, :] = jnp.where(is0 | is1, 1.0, 0.0)
        gate = jnp.where(is0, gate0, 0.0) + jnp.where(is1, gate1, 0.0)
        gates[rows, :] = jnp.broadcast_to(jnp.sum(gate, axis=1, keepdims=True), (CAP, TOK))

    def fwd(i):
        rows = pl.ds(i * CAP, CAP)
        return pltpu.make_async_remote_copy(
            sent.at[:, rows, :], arrived.at[p, :, rows, :], a_send.at[i], a_recv.at[i],
            device_id=at(0, *MESSAGES[i]), device_id_type=MESH,
        )

    own_rows = pl.ds(SELF * CAP, CAP)
    own_copy = pltpu.make_async_copy(
        sent.at[:, own_rows, :], arrived.at[p, :, own_rows, :], self_sem
    )

    for copy in ins:
        copy.wait()
    for ch in range(CHUNKS):
        rows = pl.ds(ch * CROWS, CROWS)
        pick = onehot[rows, :].astype(BF16)
        sent[0, rows, :] = nn(pick, tok[0]).astype(BF16)
        gate = gates[rows, 0:1]
        sent[1, rows, :] = (nn(pick, tok[1]) * gate).astype(BF16)
        if ch == 0:
            pl.semaphore_wait(barrier, len(peers))
        for i in range(ch * PER, (ch + 1) * PER):
            if i == SELF:
                own_copy.start()
            else:
                fwd(i).start()

    def sides(src, dst, ch, send, recv):
        rows = pl.ds(ch * CROWS, CROWS)
        copies = []
        for side, dx in enumerate((1, -1)):
            cols = pl.ds(side * QUARTER, QUARTER)
            copies.append(
                pltpu.make_async_remote_copy(
                    src(rows, cols), dst(rows, cols), send.at[2 * ch + side], recv.at[2 * ch + side],
                    device_id=at(dx, 0, 0, 0), device_id_type=MESH,
                )
            )
        return copies

    def spread(ch):
        ref = lambda rows, cols: arrived.at[p, :, rows, cols]
        return sides(ref, ref, ch, x_send, x_recv)

    def gather_recv(ch):
        ref = lambda rows, cols: arrived.at[q, :, rows, cols]
        return sides(ref, ref, ch, x_send, x_recv)

    def parts(ch):
        return sides(
            lambda rows, cols: part_out.at[rows, cols],
            lambda rows, cols: part_in.at[rows, cols], ch, p_send, p_recv,
        )

    def back(i):
        dy, dz, dc = MESSAGES[i]
        rows = pl.ds(i * CAP, CAP)
        return pltpu.make_async_remote_copy(
            summed.at[rows, :], returned.at[rows, :], r_send.at[i], r_recv.at[i],
            device_id=at(0, -dy, -dz, dc), device_id_type=MESH,
        )

    def take_in(ch):
        for i in range(ch * PER, (ch + 1) * PER):
            if i == SELF:
                own_copy.wait()
            else:
                fwd(i).wait_recv()
        for copy in spread(ch):
            copy.start()

    def compute(ch):
        for copy in gather_recv(ch):
            copy.wait_recv()
        rows = pl.ds(ch * CROWS, CROWS)
        gate_pre = nt(arrived[0, 0, rows, :], weights[0, 0]) + nt(arrived[1, 0, rows, :], weights[0, 1])
        up_pre = nt(arrived[0, 0, rows, :], weights[1, 0]) + nt(arrived[1, 0, rows, :], weights[1, 1])
        act_grad = nt(arrived[0, 1, rows, :], weights[2, 0]) + nt(arrived[1, 1, rows, :], weights[2, 1])
        s = jax.nn.sigmoid(gate_pre)
        swish = gate_pre * s
        act[rows, :] = (swish * up_pre).astype(BF16)
        gate_grad = (act_grad * up_pre * (s * (1.0 + gate_pre * (1.0 - s)))).astype(BF16)
        up_grad = (act_grad * swish).astype(BF16)
        ggrad[rows, :] = gate_grad
        ugrad[rows, :] = up_grad
        part_out[rows, :] = (nn(gate_grad, weights[0, q]) + nn(up_grad, weights[1, q])).astype(BF16)
        for copy in parts(ch):
            copy.start()
        part_own[rows, :] = nn(gate_grad, weights[0, p]) + nn(up_grad, weights[1, p])

    self_back = pltpu.make_async_copy(summed.at[own_rows, :], returned.at[own_rows, :], self_sem)

    def give_back(ch):
        for copy in parts(ch):
            copy.wait_recv()
        rows = pl.ds(ch * CROWS, CROWS)
        summed[rows, :] = (part_own[rows, :] + part_in[rows, :].astype(F32)).astype(BF16)
        for i in range(ch * PER, (ch + 1) * PER):
            if i == SELF:
                self_back.start()
            else:
                back(i).start()

    take_in(0)
    for copy in w_ins:
        copy.wait()
    for ch in range(1, CHUNKS + 2):
        if ch < CHUNKS:
            take_in(ch)
        if ch - 1 < CHUNKS:
            compute(ch - 1)
        if ch >= 2:
            give_back(ch - 2)

    outs = (gg_hbm, gu_hbm, gd_hbm)

    def grad_copy(i, b):
        return pltpu.make_async_copy(
            grads.at[i, b], outs[i].at[:, pl.ds(pl.multiple_of(b * BLOCK, BLOCK), BLOCK)], g_sem.at[i, b]
        )

    @pl.loop(0, 8)
    def _(b):
        half, cols = b % 2, pl.ds(pl.multiple_of((b // 2) * BLOCK, BLOCK), BLOCK)
        inputs = arrived[half, 0, :, cols]
        grads[0, b] = tn(ggrad[...], inputs).astype(BF16)
        grad_copy(0, b).start()
        grads[1, b] = tn(ugrad[...], inputs).astype(BF16)
        grad_copy(1, b).start()
        grads[2, b] = tn(act[...], arrived[half, 1, :, cols]).astype(BF16)
        grad_copy(2, b).start()

    self_back.wait()
    for i in REMOTE:
        back(i).wait_recv()
    fin_peers = ((2, 0, 0, 0), (0, 0, 4, 0), (2, 0, 4, 0))
    j_own = 2 * h + x // 2

    def fin(d):
        j_x, j_z = (x // 2 + d % 2) % 2, (h + d // 2) % 2
        return pltpu.make_async_remote_copy(
            fin_out.at[2 * j_z + j_x], fin_in.at[d - 1], f_send.at[d - 1], f_recv.at[d - 1],
            device_id=at(*fin_peers[d - 1]), device_id_type=MESH,
        )

    pick = onehot[...].T.astype(BF16)
    for j in range(4):
        block = nn(pick, returned[:, pl.ds(j * BLOCK, BLOCK)])
        combined[j] = block
        fin_out[j] = block.astype(BF16)
    for d in (3, 2, 1):
        fin(d).start()
    total = combined[j_own]
    for d in (1, 2, 3):
        fin(d).wait_recv()
        total += fin_in[d - 1].astype(F32)
    gt_ref[...] = total.astype(BF16)

    for i in REMOTE:
        fwd(i).wait_send()
        back(i).wait_send()
    for ch in range(CHUNKS):
        for copy in spread(ch) + parts(ch):
            copy.wait_send()
    for d in (1, 2, 3):
        fin(d).wait_send()

    @pl.loop(0, 8)
    def _(b):
        for i in range(3):
            grad_copy(i, b).wait()


def local(tokens_x, cotangent, expert_ids, gate_weights, w_gate, w_up, w_down):
    routes = jnp.concatenate([expert_ids.astype(F32), gate_weights], axis=1).T
    vmem = pl.BlockSpec(memory_space=pltpu.VMEM)
    anywhere = pl.BlockSpec(memory_space=pl.ANY)
    dma = pltpu.SemaphoreType.DMA
    grad = jax.ShapeDtypeStruct((FF, D), BF16)
    grad_tokens, grad_gate, grad_up, grad_down = pl.pallas_call(
        kernel,
        out_shape=(jax.ShapeDtypeStruct((TOK, BLOCK), BF16), grad, grad, grad),
        in_specs=[vmem] + [anywhere] * 5,
        out_specs=(vmem, anywhere, anywhere, anywhere),
        scratch_shapes=[
            pltpu.VMEM((2, TOK, HALF), BF16),
            pltpu.VMEM((3, 2, FF, HALF), BF16),
            pltpu.VMEM((ROWS, TOK), F32),
            pltpu.VMEM((ROWS, TOK), F32),
            pltpu.VMEM((2, ROWS, HALF), BF16),
            pltpu.VMEM((2, 2, ROWS, HALF), BF16),
            pltpu.VMEM((ROWS, FF), BF16),
            pltpu.VMEM((ROWS, FF), BF16),
            pltpu.VMEM((ROWS, FF), BF16),
            pltpu.VMEM((ROWS, HALF), F32),
            pltpu.VMEM((ROWS, HALF), BF16),
            pltpu.VMEM((ROWS, HALF), BF16),
            pltpu.VMEM((ROWS, HALF), BF16),
            pltpu.VMEM((ROWS, HALF), BF16),
            pltpu.VMEM((4, TOK, BLOCK), F32),
            pltpu.VMEM((4, TOK, BLOCK), BF16),
            pltpu.VMEM((3, TOK, BLOCK), BF16),
            pltpu.VMEM((3, 8, FF, BLOCK), BF16),
            dma((8,)), dma((24,)), dma,
            dma((EXPERTS,)), dma((EXPERTS,)),
            dma((2 * CHUNKS,)), dma((2 * CHUNKS,)),
            dma((2 * CHUNKS,)), dma((2 * CHUNKS,)),
            dma((EXPERTS,)), dma((EXPERTS,)),
            dma((3,)), dma((3,)), dma((3, 8)),
        ],
        name="expert_backward",
        compiler_params=pltpu.CompilerParams(
            collective_id=0, has_side_effects=True, vmem_limit_bytes=56 * 2**20
        ),
    )(routes, tokens_x, cotangent, w_gate[0], w_up[0], w_down[0])
    return grad_tokens, grad_gate[None], grad_up[None], grad_down[None]


def solution(mesh):
    placed = (
        P("expert", None),
        P("expert", None),
        P("expert", None),
        P("expert", None),
        P("expert", "dp", None),
        P("expert", "dp", None),
        P("expert", "dp", None),
    )
    return jax.shard_map(
        local,
        mesh=mesh,
        in_specs=placed,
        out_specs=(
            P("expert", "dp"),
            P("expert", "dp", None),
            P("expert", "dp", None),
            P("expert", "dp", None),
        ),
        check_vma=False,
    )
```

```python
import functools

import jax
import jax.numpy as jnp
from jax import lax
from jax.experimental import pallas as pl
from jax.experimental.pallas import tpu as pltpu
from jax.sharding import PartitionSpec as P

MESH = pl.DeviceIdType.MESH
F32, BF16 = jnp.float32, jnp.bfloat16
D = 4096
HALF = 2048
QUARTER = 1024
BLOCK = 512
FF = 192
TOK = 128
CAP = 16
EXPERTS = 32
ROWS = EXPERTS * CAP
SIZES = (8, 8, 8, 8)
CHUNKS = len(SIZES)
FIRST = tuple(sum(SIZES[:ch]) for ch in range(CHUNKS))

Z_C = ((1, 0), (-1, 0), (2, 0), (0, 1), (-1, 1), (1, 1), (-2, 1), (0, 0))
ON_CHIP = ((0, 0, 1), (0, 0, 0))
MESSAGES = tuple(
    (dy,) + Z_C[(k + 2 * n) % 8]
    for k in range(8)
    for n, dy in enumerate((1, 3, 2, 0))
    if (dy,) + Z_C[(k + 2 * n) % 8] not in ON_CHIP
) + ON_CHIP
CORE, SELF = EXPERTS - 2, EXPERTS - 1
REMOTE = tuple(range(SELF))


def nt(left, right):
    return lax.dot_general(left, right, (((1,), (1,)), ((), ())), preferred_element_type=F32)


def nn(left, right):
    return lax.dot_general(left, right, (((1,), (0,)), ((), ())), preferred_element_type=F32)


def tn(left, right):
    return lax.dot_general(left, right, (((0,), (0,)), ((), ())), preferred_element_type=F32)


def ranks(routes):
    ids0, ids1 = routes[0:1, :], routes[1:2, :]
    expert_row = lax.broadcasted_iota(jnp.int32, (EXPERTS, TOK), 0).astype(F32)
    earlier = (
        lax.broadcasted_iota(jnp.int32, (TOK, TOK), 0)
        < lax.broadcasted_iota(jnp.int32, (TOK, TOK), 1)
    )
    earlier = jnp.where(earlier, 1.0, 0.0).astype(BF16)
    hot0 = jnp.where(expert_row == ids0, 1.0, 0.0)
    hot1 = jnp.where(expert_row == ids1, 1.0, 0.0)
    before0 = nn(hot0.astype(BF16), earlier)
    before1 = nn(hot1.astype(BF16), earlier) + jnp.sum(hot0, axis=1, keepdims=True)
    return (
        jnp.sum(hot0 * before0, axis=0, keepdims=True),
        jnp.sum(hot1 * before1, axis=0, keepdims=True),
    )


def kernel(
    ids_ref, gate_ref, tok_hbm, cot_hbm, wg_hbm, wu_hbm, wd_hbm,
    gt_ref, gg_hbm, gu_hbm, gd_hbm,
    tok, tok_q, weights, onehot, gates, sent, sent_q, arrived, slope, swish, act, ggrad, ugrad,
    part_own, part_out, part_in, summed, returned, combined, fin_out, fin_in, fin_out2, fin_in2, grads,
    tok_sem, tok_q_sem, w_sem, self_sem,
    a_send, a_recv, k_send, k_recv, x_send, x_recv, p_send, p_recv, r_send, r_recv, s_send, s_recv, g_sem,
):
    dp, ex = lax.axis_index("dp"), lax.axis_index("expert")
    h, x = dp // 4, dp % 4
    y, l, c = ex // 8, (ex // 2) % 4, ex % 2
    z = h * 4 + l
    p = x % 2
    q = 1 - p

    def at(dx, dy, dz, dc):
        zz = (z + dz + 8) % 8
        return (
            (zz // 4) * 4 + (x + dx + 4) % 4,
            ((y + dy + 4) % 4) * 8 + (zz % 4) * 2 + (c + dc) % 2,
        )

    def remote(src, dst, send, recv, *offset):
        return pltpu.make_async_remote_copy(
            src, dst, send, recv, device_id=at(*offset), device_id_type=MESH
        )

    ins, q_ins, w_ins = [], [], []
    for i, src in enumerate((tok_hbm, cot_hbm)):
        for j in range(4):
            to = pl.ds(j * BLOCK, BLOCK)
            cols = pl.ds(pl.multiple_of((2 * j + p) * BLOCK, BLOCK), BLOCK)
            ins.append(pltpu.make_async_copy(src.at[:, cols], tok.at[i, :, to], tok_sem.at[4 * i + j]))
            cols = pl.ds(pl.multiple_of((2 * j + q) * BLOCK, BLOCK), BLOCK)
            q_ins.append(pltpu.make_async_copy(src.at[:, cols], tok_q.at[i, :, to], tok_q_sem.at[4 * i + j]))
    for i, src in enumerate((wg_hbm, wu_hbm, wd_hbm)):
        for b in range(8):
            to = pl.ds((b // 2) * BLOCK, BLOCK)
            w_ins.append(
                pltpu.make_async_copy(
                    src.at[:, pl.ds(b * BLOCK, BLOCK)], weights.at[i, b % 2, :, to], w_sem.at[8 * i + b]
                )
            )
    for copy in ins + q_ins + w_ins:
        copy.start()

    barrier = pltpu.get_barrier_semaphore()
    peers = [(0,) + MESSAGES[i] for i in REMOTE]
    peers += [(0, dy, -dz, dc) for dy, dz, dc in MESSAGES if abs(dz) == 2]
    peers += [(1, 0, 0, 0), (-1, 0, 0, 0), (2, 0, 0, 0), (0, 0, 4, 0)]
    for peer in peers:
        pl.semaphore_signal(barrier, inc=1, device_id=at(*peer), device_id_type=MESH)

    route = jnp.concatenate([ids_ref[...].astype(F32), gate_ref[...]], axis=0)
    rank0, rank1 = ranks(route)
    slot_row = lax.broadcasted_iota(jnp.int32, (CAP, TOK), 0).astype(F32)

    def slots(ch):
        for i in range(FIRST[ch], FIRST[ch] + SIZES[ch]):
            dy, dz, dc = MESSAGES[i]
            expert = (((y + dy) % 4) * 8 + ((l + dz + 4) % 4) * 2 + (c + dc) % 2).astype(F32)
            is0 = (slot_row == rank0) & (route[0:1, :] == expert)
            is1 = (slot_row == rank1) & (route[1:2, :] == expert)
            rows = pl.ds(i * CAP, CAP)
            onehot[rows, :] = jnp.where(is0 | is1, 1.0, 0.0)
            gate = jnp.where(is0, route[2:3, :], 0.0) + jnp.where(is1, route[3:4, :], 0.0)
            gates[rows, :] = jnp.broadcast_to(jnp.sum(gate, axis=1, keepdims=True), (CAP, TOK))

    def chunk_rows(ch, less=0):
        return pl.ds(FIRST[ch] * CAP, SIZES[ch] * CAP - less)

    def out_copy(i, kind):
        rows = pl.ds(i * CAP, CAP)
        return remote(
            sent.at[kind, rows], arrived.at[p, kind, rows], a_send.at[kind, i], a_recv.at[kind, i], 0, *MESSAGES[i]
        )

    def core_copy(kind):
        return remote(
            sent_q.at[kind], arrived.at[q, kind, pl.ds(CORE * CAP, CAP)], k_send.at[kind], k_recv.at[kind], 0, 0, 0, 1
        )

    def send_slots(ch, kind):
        rows = chunk_rows(ch)
        picked = nn(onehot[rows, :].astype(BF16), tok[kind])
        if kind == 1:
            picked = picked * gates[rows, 0:1]
        picked = picked.astype(BF16)
        sent[kind, rows, :] = picked
        for i in range(FIRST[ch], FIRST[ch] + SIZES[ch]):
            if i == SELF:
                arrived[p, kind, pl.ds(SELF * CAP, CAP), :] = picked[(SELF - FIRST[ch]) * CAP :]
            else:
                out_copy(i, kind).start()

    def send_local(kind):
        rows = pl.ds(CORE * CAP, 2 * CAP)
        picked = nn(onehot[rows, :].astype(BF16), tok_q[kind])
        if kind == 1:
            picked = picked * gates[rows, 0:1]
        picked = picked.astype(BF16)
        sent_q[kind] = picked[0:CAP]
        core_copy(kind).start()
        arrived[q, kind, pl.ds(SELF * CAP, CAP), :] = picked[CAP:]

    def sides(rows, src, dst, send, recv):
        return [
            remote(src(rows, cols), dst(rows, cols), send(side), recv(side), dx, 0, 0, 0)
            for side, dx, cols in ((0, 1, pl.ds(0, QUARTER)), (1, -1, pl.ds(QUARTER, QUARTER)))
        ]

    def spread(ch, kind, half):
        ref = lambda rows, cols: arrived.at[half, kind, rows, cols]
        rows = chunk_rows(ch, 2 * CAP if ch == CHUNKS - 1 else 0)
        return sides(
            rows, ref, ref, lambda side: x_send.at[ch, kind, side], lambda side: x_recv.at[ch, kind, side]
        )

    def forward(ch, kind):
        for i in range(FIRST[ch], FIRST[ch] + SIZES[ch]):
            if i not in (CORE, SELF):
                out_copy(i, kind).wait_recv()
        for copy in spread(ch, kind, p):
            copy.start()

    def parts(ch):
        return sides(
            chunk_rows(ch), lambda rows, cols: part_out.at[rows, cols], lambda rows, cols: part_in.at[rows, cols],
            lambda side: p_send.at[ch, side], lambda side: p_recv.at[ch, side],
        )

    def wait_rows(ch, kind):
        for copy in spread(ch, kind, q):
            copy.wait_recv()
        if ch == CHUNKS - 1:
            out_copy(CORE, kind).wait_recv()
            core_copy(kind).wait_recv()

    def compute_tokens(ch):
        wait_rows(ch, 0)
        rows = chunk_rows(ch)
        gate_pre = nt(arrived[0, 0, rows, :], weights[0, 0]) + nt(arrived[1, 0, rows, :], weights[0, 1])
        up_pre = nt(arrived[0, 0, rows, :], weights[1, 0]) + nt(arrived[1, 0, rows, :], weights[1, 1])
        s = jax.nn.sigmoid(gate_pre)
        value = gate_pre * s
        act[rows, :] = (value * up_pre).astype(BF16)
        swish[rows, :] = value
        slope[rows, :] = up_pre * (s * (1.0 + gate_pre * (1.0 - s)))

    def compute_cotangents(ch):
        wait_rows(ch, 1)
        rows = chunk_rows(ch)
        act_grad = nt(arrived[0, 1, rows, :], weights[2, 0]) + nt(arrived[1, 1, rows, :], weights[2, 1])
        gate_grad = (act_grad * slope[rows, :]).astype(BF16)
        up_grad = (act_grad * swish[rows, :]).astype(BF16)
        ggrad[rows, :] = gate_grad
        ugrad[rows, :] = up_grad
        part_out[rows, :] = (nn(gate_grad, weights[0, q]) + nn(up_grad, weights[1, q])).astype(BF16)
        for copy in parts(ch):
            copy.start()
        part_own[rows, :] = nn(gate_grad, weights[0, p]) + nn(up_grad, weights[1, p])

    def back(i):
        dy, dz, dc = MESSAGES[i]
        rows = pl.ds(i * CAP, CAP)
        return remote(summed.at[rows], returned.at[rows], r_send.at[i], r_recv.at[i], 0, -dy, -dz, dc)

    own_rows = pl.ds(SELF * CAP, CAP)
    self_back = pltpu.make_async_copy(summed.at[own_rows], returned.at[own_rows], self_sem)

    def give_back(ch):
        for copy in parts(ch):
            copy.wait_recv()
        rows = chunk_rows(ch)
        summed[rows, :] = (part_own[rows, :] + part_in[rows, :].astype(F32)).astype(BF16)
        for i in range(FIRST[ch], FIRST[ch] + SIZES[ch]):
            if i == SELF:
                self_back.start()
            else:
                back(i).start()

    slots(0)
    for copy in ins:
        copy.wait()
    pl.semaphore_wait(barrier, len(peers))
    for ch in range(CHUNKS):
        if ch:
            slots(ch)
        send_slots(ch, 0)
        send_slots(ch, 1)
    for copy in q_ins:
        copy.wait()
    send_local(0)
    send_local(1)
    pick = onehot[...].T.astype(BF16)
    for ch in range(CHUNKS):
        forward(ch, 0)
        if ch == 0:
            for copy in w_ins:
                copy.wait()
        else:
            compute_cotangents(ch - 1)
        forward(ch, 1)
        compute_tokens(ch)
        if ch:
            give_back(ch - 1)
    compute_cotangents(CHUNKS - 1)
    give_back(CHUNKS - 1)

    outs = (gg_hbm, gu_hbm, gd_hbm)

    def grad_copy(i, b):
        return pltpu.make_async_copy(
            grads.at[i, b], outs[i].at[:, pl.ds(pl.multiple_of(b * BLOCK, BLOCK), BLOCK)], g_sem.at[i, b]
        )

    @pl.loop(0, 8)
    def _(b):
        half, cols = b % 2, pl.ds(pl.multiple_of((b // 2) * BLOCK, BLOCK), BLOCK)
        inputs = arrived[half, 0, :, cols]
        grads[0, b] = tn(ggrad[...], inputs).astype(BF16)
        grad_copy(0, b).start()
        grads[1, b] = tn(ugrad[...], inputs).astype(BF16)
        grad_copy(1, b).start()
        grads[2, b] = tn(act[...], arrived[half, 1, :, cols]).astype(BF16)
        grad_copy(2, b).start()

    self_back.wait()
    for i in REMOTE:
        back(i).wait_recv()

    j_x, j_z = x // 2, h

    def fin_x(k):
        return remote(fin_out.at[k], fin_in.at[k], s_send.at[k], s_recv.at[k], 2, 0, 0, 0)

    fin_z = remote(fin_out2, fin_in2, s_send.at[2], s_recv.at[2], 0, 0, 4, 0)

    def token_block(b_z, b_x):
        cols = pl.ds(pl.multiple_of((2 * b_z + b_x) * BLOCK, BLOCK), BLOCK)
        return nn(pick, returned[:, cols])

    for k, b_z in enumerate((1 - j_z, j_z)):
        fin_out[k] = token_block(b_z, 1 - j_x).astype(BF16)
        fin_x(k).start()
    for k, b_z in enumerate((1 - j_z, j_z)):
        combined[k] = token_block(b_z, j_x)
    fin_x(0).wait_recv()
    fin_out2[...] = (combined[0] + fin_in[0].astype(F32)).astype(BF16)
    fin_z.start()
    fin_x(1).wait_recv()
    total = combined[1] + fin_in[1].astype(F32)
    fin_z.wait_recv()
    gt_ref[...] = (total + fin_in2[...].astype(F32)).astype(BF16)

    for i in REMOTE:
        out_copy(i, 0).wait_send()
        out_copy(i, 1).wait_send()
        back(i).wait_send()
    for kind in range(2):
        core_copy(kind).wait_send()
    for ch in range(CHUNKS):
        for copy in spread(ch, 0, p) + spread(ch, 1, p) + parts(ch):
            copy.wait_send()
    for copy in (fin_x(0), fin_x(1), fin_z):
        copy.wait_send()

    @pl.loop(0, 8)
    def _(b):
        for i in range(3):
            grad_copy(i, b).wait()


PIECES = 2


def finish(*refs):
    ins, outs, held, in_sem, out_sem = refs[:3], refs[3:6], refs[6], refs[7], refs[8]
    copies = []
    for i in range(3):
        for k in range(PIECES):
            rows = pl.ds(k * (FF // PIECES), FF // PIECES)
            copies.append((
                pltpu.make_async_copy(ins[i].at[rows], held.at[i, rows], in_sem.at[i, k]),
                pltpu.make_async_copy(held.at[i, rows], outs[i].at[rows], out_sem.at[i, k]),
            ))
    for copy, _ in copies:
        copy.start()
    for copy, on in copies:
        copy.wait()
        on.start()
    for _, on in copies:
        on.wait()


def local(tokens_x, cotangent, expert_ids, gate_weights, w_gate, w_up, w_down):
    vmem = pl.BlockSpec(memory_space=pltpu.VMEM)
    anywhere = pl.BlockSpec(memory_space=pl.ANY)
    dma = pltpu.SemaphoreType.DMA
    grad = jax.ShapeDtypeStruct((FF, D), BF16)
    grad_tokens, *grads = pl.pallas_call(
        kernel,
        out_shape=(jax.ShapeDtypeStruct((TOK, BLOCK), BF16), grad, grad, grad),
        in_specs=[vmem] * 2 + [anywhere] * 5,
        out_specs=(vmem, anywhere, anywhere, anywhere),
        scratch_shapes=[
            pltpu.VMEM((2, TOK, HALF), BF16),
            pltpu.VMEM((2, TOK, HALF), BF16),
            pltpu.VMEM((3, 2, FF, HALF), BF16),
            pltpu.VMEM((ROWS, TOK), F32),
            pltpu.VMEM((ROWS, TOK), F32),
            pltpu.VMEM((2, ROWS, HALF), BF16),
            pltpu.VMEM((2, CAP, HALF), BF16),
            pltpu.VMEM((2, 2, ROWS, HALF), BF16),
            pltpu.VMEM((ROWS, FF), F32),
            pltpu.VMEM((ROWS, FF), F32),
            pltpu.VMEM((ROWS, FF), BF16),
            pltpu.VMEM((ROWS, FF), BF16),
            pltpu.VMEM((ROWS, FF), BF16),
            pltpu.VMEM((ROWS, HALF), F32),
            pltpu.VMEM((ROWS, HALF), BF16),
            pltpu.VMEM((ROWS, HALF), BF16),
            pltpu.VMEM((ROWS, HALF), BF16),
            pltpu.VMEM((ROWS, HALF), BF16),
            pltpu.VMEM((2, TOK, BLOCK), F32),
            pltpu.VMEM((2, TOK, BLOCK), BF16),
            pltpu.VMEM((2, TOK, BLOCK), BF16),
            pltpu.VMEM((TOK, BLOCK), BF16),
            pltpu.VMEM((TOK, BLOCK), BF16),
            pltpu.VMEM((3, 8, FF, BLOCK), BF16),
            dma((8,)), dma((8,)), dma((24,)), dma,
            dma((2, EXPERTS)), dma((2, EXPERTS)), dma((2,)), dma((2,)),
            dma((CHUNKS, 2, 2)), dma((CHUNKS, 2, 2)), dma((CHUNKS, 2)), dma((CHUNKS, 2)),
            dma((EXPERTS,)), dma((EXPERTS,)), dma((3,)), dma((3,)), dma((3, 8)),
        ],
        name="expert_backward",
        compiler_params=pltpu.CompilerParams(
            collective_id=0, has_side_effects=True, vmem_limit_bytes=56 * 2**20
        ),
    )(expert_ids.T, gate_weights.T, tokens_x, cotangent, w_gate[0], w_up[0], w_down[0])
    grad_gate, grad_up, grad_down = pl.pallas_call(
        finish,
        out_shape=(grad, grad, grad),
        in_specs=[anywhere] * 3,
        out_specs=[anywhere] * 3,
        scratch_shapes=[pltpu.VMEM((3, FF, D), BF16), dma((3, PIECES)), dma((3, PIECES))],
        name="finish",
        compiler_params=pltpu.CompilerParams(vmem_limit_bytes=56 * 2**20),
    )(*grads)
    return grad_tokens, grad_gate[None], grad_up[None], grad_down[None]


def solution(mesh):
    placed = (
        P("expert", None),
        P("expert", None),
        P("expert", None),
        P("expert", None),
        P("expert", "dp", None),
        P("expert", "dp", None),
        P("expert", "dp", None),
    )
    return jax.shard_map(
        local,
        mesh=mesh,
        in_specs=placed,
        out_specs=(
            P("expert", "dp"),
            P("expert", "dp", None),
            P("expert", "dp", None),
            P("expert", "dp", None),
        ),
        check_vma=False,
    )
```

```python
import functools

import jax
import jax.numpy as jnp
from jax import lax
from jax.experimental import pallas as pl
from jax.experimental.pallas import tpu as pltpu
from jax.sharding import PartitionSpec as P

MESH = pl.DeviceIdType.MESH
F32, BF16 = jnp.float32, jnp.bfloat16
D = 4096
HALF = 2048
QUARTER = 1024
BLOCK = 512
FF = 192
TOK = 128
CAP = 16
EXPERTS = 32
ROWS = EXPERTS * CAP
SIZES = (4,4,4,4,4,4,4,4)
CHUNKS = len(SIZES)
FIRST = tuple(sum(SIZES[:ch]) for ch in range(CHUNKS))

Z_C = ((1, 0), (-1, 0), (2, 0), (0, 1), (-1, 1), (1, 1), (-2, 1), (0, 0))
ON_CHIP = ((0, 0, 1), (0, 0, 0))
MESSAGES = tuple(
    (dy,) + Z_C[(k + 2 * n) % 8]
    for k in range(8)
    for n, dy in enumerate((1, 2, 3, 0))
    if (dy,) + Z_C[(k + 2 * n) % 8] not in ON_CHIP
) + ON_CHIP
CORE, SELF = EXPERTS - 2, EXPERTS - 1
REMOTE = tuple(range(SELF))


def nt(left, right):
    return lax.dot_general(left, right, (((1,), (1,)), ((), ())), preferred_element_type=F32)


def nn(left, right):
    return lax.dot_general(left, right, (((1,), (0,)), ((), ())), preferred_element_type=F32)


def tn(left, right):
    return lax.dot_general(left, right, (((0,), (0,)), ((), ())), preferred_element_type=F32)


def ranks(routes):
    ids0, ids1 = routes[0:1, :], routes[1:2, :]
    expert_row = lax.broadcasted_iota(jnp.int32, (EXPERTS, TOK), 0).astype(F32)
    earlier = (
        lax.broadcasted_iota(jnp.int32, (TOK, TOK), 0)
        < lax.broadcasted_iota(jnp.int32, (TOK, TOK), 1)
    )
    earlier = jnp.where(earlier, 1.0, 0.0).astype(BF16)
    hot0 = jnp.where(expert_row == ids0, 1.0, 0.0)
    hot1 = jnp.where(expert_row == ids1, 1.0, 0.0)
    before0 = nn(hot0.astype(BF16), earlier)
    before1 = nn(hot1.astype(BF16), earlier) + jnp.sum(hot0, axis=1, keepdims=True)
    return (
        jnp.sum(hot0 * before0, axis=0, keepdims=True),
        jnp.sum(hot1 * before1, axis=0, keepdims=True),
    )


def kernel(
    ids_ref, gate_ref, tok_hbm, cot_hbm, wg_hbm, wu_hbm, wd_hbm,
    gt_ref, gg_hbm, gu_hbm, gd_hbm,
    tok, tok_q, weights, onehot, gates, sent, sent_q, arrived, slope, swish, act, ggrad, ugrad,
    part_own, part_out, part_in, summed, returned, combined, fin_out, fin_in, fin_out2, fin_in2, grads,
    tok_sem, tok_q_sem, w_sem, self_sem,
    a_send, a_recv, k_send, k_recv, x_send, x_recv, p_send, p_recv, r_send, r_recv, s_send, s_recv, g_sem,
):
    dp, ex = lax.axis_index("dp"), lax.axis_index("expert")
    h, x = dp // 4, dp % 4
    y, l, c = ex // 8, (ex // 2) % 4, ex % 2
    z = h * 4 + l
    p = x % 2
    q = 1 - p
    turn = 1 - 2 * c

    def at(dx, dy, dz, dc):
        zz = (z + dz + 8) % 8
        return (
            (zz // 4) * 4 + (x + dx + 4) % 4,
            ((y + dy + 4) % 4) * 8 + (zz % 4) * 2 + (c + dc) % 2,
        )

    def remote(src, dst, send, recv, *offset):
        return pltpu.make_async_remote_copy(
            src, dst, send, recv, device_id=at(*offset), device_id_type=MESH
        )

    ins, q_ins, w_ins = [], [], []
    for i, src in enumerate((tok_hbm, cot_hbm)):
        for j in range(4):
            to = pl.ds(j * BLOCK, BLOCK)
            cols = pl.ds(pl.multiple_of((2 * j + p) * BLOCK, BLOCK), BLOCK)
            ins.append(pltpu.make_async_copy(src.at[:, cols], tok.at[i, :, to], tok_sem.at[4 * i + j]))
            cols = pl.ds(pl.multiple_of((2 * j + q) * BLOCK, BLOCK), BLOCK)
            q_ins.append(pltpu.make_async_copy(src.at[:, cols], tok_q.at[i, :, to], tok_q_sem.at[4 * i + j]))
    for i, src in enumerate((wg_hbm, wu_hbm, wd_hbm)):
        for b in range(8):
            to = pl.ds((b // 2) * BLOCK, BLOCK)
            w_ins.append(
                pltpu.make_async_copy(
                    src.at[:, pl.ds(b * BLOCK, BLOCK)], weights.at[i, b % 2, :, to], w_sem.at[8 * i + b]
                )
            )
    for copy in ins + q_ins + w_ins:
        copy.start()

    barrier = pltpu.get_barrier_semaphore()
    peers = [(0,) + MESSAGES[i] for i in REMOTE]
    peers += [(0, dy, -dz, dc) for dy, dz, dc in MESSAGES if abs(dz) == 2]
    peers += [(1, 0, 0, 0), (-1, 0, 0, 0), (2, 0, 0, 0), (0, 0, 4, 0)]
    for peer in peers:
        pl.semaphore_signal(barrier, inc=1, device_id=at(*peer), device_id_type=MESH)

    route = jnp.concatenate([ids_ref[...].astype(F32), gate_ref[...]], axis=0)
    rank0, rank1 = ranks(route)
    slot_row = lax.broadcasted_iota(jnp.int32, (CAP, TOK), 0).astype(F32)

    def slots(ch):
        for i in range(FIRST[ch], FIRST[ch] + SIZES[ch]):
            dy, dz, dc = MESSAGES[i]
            expert = ((y + turn * dy + 4) % 4) * 8 + ((l + turn * dz + 4) % 4) * 2 + (c + dc) % 2
            expert = expert.astype(F32)
            is0 = (slot_row == rank0) & (route[0:1, :] == expert)
            is1 = (slot_row == rank1) & (route[1:2, :] == expert)
            rows = pl.ds(i * CAP, CAP)
            onehot[rows, :] = jnp.where(is0 | is1, 1.0, 0.0)
            gate = jnp.where(is0, route[2:3, :], 0.0) + jnp.where(is1, route[3:4, :], 0.0)
            gates[rows, :] = jnp.broadcast_to(jnp.sum(gate, axis=1, keepdims=True), (CAP, TOK))

    def chunk_rows(ch, less=0):
        return pl.ds(FIRST[ch] * CAP, SIZES[ch] * CAP - less)

    def out_copy(i, kind):
        dy, dz, dc = MESSAGES[i]
        rows = pl.ds(i * CAP, CAP)
        return remote(
            sent.at[kind, rows], arrived.at[p, kind, rows], a_send.at[kind, i], a_recv.at[kind, i], 0, turn * dy, turn * dz, dc
        )

    def core_copy(kind):
        return remote(
            sent_q.at[kind], arrived.at[q, kind, pl.ds(CORE * CAP, CAP)], k_send.at[kind], k_recv.at[kind], 0, 0, 0, 1
        )

    def send_slots(ch, kind):
        rows = chunk_rows(ch)
        picked = nn(onehot[rows, :].astype(BF16), tok[kind])
        if kind == 1:
            picked = picked * gates[rows, 0:1]
        picked = picked.astype(BF16)
        sent[kind, rows, :] = picked
        for i in range(FIRST[ch], FIRST[ch] + SIZES[ch]):
            if i == SELF:
                arrived[p, kind, pl.ds(SELF * CAP, CAP), :] = picked[(SELF - FIRST[ch]) * CAP :]
            else:
                out_copy(i, kind).start()

    def send_local(kind):
        rows = pl.ds(CORE * CAP, 2 * CAP)
        picked = nn(onehot[rows, :].astype(BF16), tok_q[kind])
        if kind == 1:
            picked = picked * gates[rows, 0:1]
        picked = picked.astype(BF16)
        sent_q[kind] = picked[0:CAP]
        core_copy(kind).start()
        arrived[q, kind, pl.ds(SELF * CAP, CAP), :] = picked[CAP:]

    def sides(rows, src, dst, send, recv):
        return [
            remote(src(rows, cols), dst(rows, cols), send(side), recv(side), dx, 0, 0, 0)
            for side, dx, cols in ((0, 1, pl.ds(0, QUARTER)), (1, -1, pl.ds(QUARTER, QUARTER)))
        ]

    def spread(ch, kind, half):
        ref = lambda rows, cols: arrived.at[half, kind, rows, cols]
        rows = chunk_rows(ch, 2 * CAP if ch == CHUNKS - 1 else 0)
        return sides(
            rows, ref, ref, lambda side: x_send.at[ch, kind, side], lambda side: x_recv.at[ch, kind, side]
        )

    def forward(ch, kind):
        for i in range(FIRST[ch], FIRST[ch] + SIZES[ch]):
            if i not in (CORE, SELF):
                out_copy(i, kind).wait_recv()
        for copy in spread(ch, kind, p):
            copy.start()

    def parts(ch):
        return sides(
            chunk_rows(ch), lambda rows, cols: part_out.at[rows, cols], lambda rows, cols: part_in.at[rows, cols],
            lambda side: p_send.at[ch, side], lambda side: p_recv.at[ch, side],
        )

    def wait_rows(ch, kind):
        for copy in spread(ch, kind, q):
            copy.wait_recv()
        if ch == CHUNKS - 1:
            out_copy(CORE, kind).wait_recv()
            core_copy(kind).wait_recv()

    def compute_tokens(ch):
        wait_rows(ch, 0)
        rows = chunk_rows(ch)
        gate_pre = nt(arrived[0, 0, rows, :], weights[0, 0]) + nt(arrived[1, 0, rows, :], weights[0, 1])
        up_pre = nt(arrived[0, 0, rows, :], weights[1, 0]) + nt(arrived[1, 0, rows, :], weights[1, 1])
        s = jax.nn.sigmoid(gate_pre)
        value = gate_pre * s
        act[rows, :] = (value * up_pre).astype(BF16)
        swish[rows, :] = value
        slope[rows, :] = up_pre * (s * (1.0 + gate_pre * (1.0 - s)))

    def compute_cotangents(ch):
        wait_rows(ch, 1)
        rows = chunk_rows(ch)
        act_grad = nt(arrived[0, 1, rows, :], weights[2, 0]) + nt(arrived[1, 1, rows, :], weights[2, 1])
        gate_grad = (act_grad * slope[rows, :]).astype(BF16)
        up_grad = (act_grad * swish[rows, :]).astype(BF16)
        ggrad[rows, :] = gate_grad
        ugrad[rows, :] = up_grad
        part_out[rows, :] = (nn(gate_grad, weights[0, q]) + nn(up_grad, weights[1, q])).astype(BF16)
        for copy in parts(ch):
            copy.start()
        part_own[rows, :] = nn(gate_grad, weights[0, p]) + nn(up_grad, weights[1, p])

    def back(i):
        dy, dz, dc = MESSAGES[i]
        rows, sign = pl.ds(i * CAP, CAP), turn if dc else -turn
        return remote(summed.at[rows], returned.at[rows], r_send.at[i], r_recv.at[i], 0, sign * dy, sign * dz, dc)

    own_rows = pl.ds(SELF * CAP, CAP)
    self_back = pltpu.make_async_copy(summed.at[own_rows], returned.at[own_rows], self_sem)

    def give_back(ch):
        for copy in parts(ch):
            copy.wait_recv()
        rows = chunk_rows(ch)
        summed[rows, :] = (part_own[rows, :] + part_in[rows, :].astype(F32)).astype(BF16)
        for i in range(FIRST[ch], FIRST[ch] + SIZES[ch]):
            if i == SELF:
                self_back.start()
            else:
                back(i).start()

    slots(0)
    for copy in ins:
        copy.wait()
    pl.semaphore_wait(barrier, len(peers))
    for ch in range(CHUNKS):
        if ch:
            slots(ch)
        send_slots(ch, 0)
        send_slots(ch, 1)
    for copy in q_ins:
        copy.wait()
    send_local(0)
    send_local(1)
    pick = onehot[...].T.astype(BF16)
    forward(0, 0)
    forward(0, 1)
    for copy in w_ins:
        copy.wait()
    for ch in range(CHUNKS):
        if ch + 1 < CHUNKS:
            forward(ch + 1, 0)
        compute_tokens(ch)
        if ch + 1 < CHUNKS:
            forward(ch + 1, 1)
        compute_cotangents(ch)
        if ch:
            give_back(ch - 1)
    give_back(CHUNKS - 1)

    outs = (gg_hbm, gu_hbm, gd_hbm)

    def grad_copy(i, b):
        return pltpu.make_async_copy(
            grads.at[i, b], outs[i].at[:, pl.ds(pl.multiple_of(b * BLOCK, BLOCK), BLOCK)], g_sem.at[i, b]
        )

    @pl.loop(0, 8)
    def _(b):
        half, cols = b % 2, pl.ds(pl.multiple_of((b // 2) * BLOCK, BLOCK), BLOCK)
        inputs = arrived[half, 0, :, cols]
        grads[0, b] = tn(ggrad[...], inputs).astype(BF16)
        grad_copy(0, b).start()
        grads[1, b] = tn(ugrad[...], inputs).astype(BF16)
        grad_copy(1, b).start()
        grads[2, b] = tn(act[...], arrived[half, 1, :, cols]).astype(BF16)
        grad_copy(2, b).start()

    self_back.wait()
    for i in REMOTE:
        back(i).wait_recv()

    j_x, j_z = x // 2, h

    def fin_x(k):
        return remote(fin_out.at[k], fin_in.at[k], s_send.at[k], s_recv.at[k], 2, 0, 0, 0)

    fin_z = remote(fin_out2, fin_in2, s_send.at[2], s_recv.at[2], 0, 0, 4, 0)

    def token_block(b_z, b_x):
        cols = pl.ds(pl.multiple_of((2 * b_z + b_x) * BLOCK, BLOCK), BLOCK)
        return nn(pick, returned[:, cols])

    for k, b_z in enumerate((1 - j_z, j_z)):
        fin_out[k] = token_block(b_z, 1 - j_x).astype(BF16)
        fin_x(k).start()
    for k, b_z in enumerate((1 - j_z, j_z)):
        combined[k] = token_block(b_z, j_x)
    fin_x(0).wait_recv()
    fin_out2[...] = (combined[0] + fin_in[0].astype(F32)).astype(BF16)
    fin_z.start()
    fin_x(1).wait_recv()
    total = combined[1] + fin_in[1].astype(F32)
    fin_z.wait_recv()
    gt_ref[...] = (total + fin_in2[...].astype(F32)).astype(BF16)

    for i in REMOTE:
        out_copy(i, 0).wait_send()
        out_copy(i, 1).wait_send()
        back(i).wait_send()
    for kind in range(2):
        core_copy(kind).wait_send()
    for ch in range(CHUNKS):
        for copy in spread(ch, 0, p) + spread(ch, 1, p) + parts(ch):
            copy.wait_send()
    for copy in (fin_x(0), fin_x(1), fin_z):
        copy.wait_send()

    @pl.loop(0, 8)
    def _(b):
        for i in range(3):
            grad_copy(i, b).wait()


PIECES = 2


def finish(*refs):
    ins, outs, held, in_sem, out_sem = refs[:3], refs[3:6], refs[6], refs[7], refs[8]
    copies = []
    for i in range(3):
        for k in range(PIECES):
            rows = pl.ds(k * (FF // PIECES), FF // PIECES)
            copies.append((
                pltpu.make_async_copy(ins[i].at[rows], held.at[i, rows], in_sem.at[i, k]),
                pltpu.make_async_copy(held.at[i, rows], outs[i].at[rows], out_sem.at[i, k]),
            ))
    for copy, _ in copies:
        copy.start()
    for copy, on in copies:
        copy.wait()
        on.start()
    for _, on in copies:
        on.wait()


def local(tokens_x, cotangent, expert_ids, gate_weights, w_gate, w_up, w_down):
    vmem = pl.BlockSpec(memory_space=pltpu.VMEM)
    anywhere = pl.BlockSpec(memory_space=pl.ANY)
    dma = pltpu.SemaphoreType.DMA
    grad = jax.ShapeDtypeStruct((FF, D), BF16)
    grad_tokens, *grads = pl.pallas_call(
        kernel,
        out_shape=(jax.ShapeDtypeStruct((TOK, BLOCK), BF16), grad, grad, grad),
        in_specs=[vmem] * 2 + [anywhere] * 5,
        out_specs=(vmem, anywhere, anywhere, anywhere),
        scratch_shapes=[
            pltpu.VMEM((2, TOK, HALF), BF16),
            pltpu.VMEM((2, TOK, HALF), BF16),
            pltpu.VMEM((3, 2, FF, HALF), BF16),
            pltpu.VMEM((ROWS, TOK), F32),
            pltpu.VMEM((ROWS, TOK), F32),
            pltpu.VMEM((2, ROWS, HALF), BF16),
            pltpu.VMEM((2, CAP, HALF), BF16),
            pltpu.VMEM((2, 2, ROWS, HALF), BF16),
            pltpu.VMEM((ROWS, FF), F32),
            pltpu.VMEM((ROWS, FF), F32),
            pltpu.VMEM((ROWS, FF), BF16),
            pltpu.VMEM((ROWS, FF), BF16),
            pltpu.VMEM((ROWS, FF), BF16),
            pltpu.VMEM((ROWS, HALF), F32),
            pltpu.VMEM((ROWS, HALF), BF16),
            pltpu.VMEM((ROWS, HALF), BF16),
            pltpu.VMEM((ROWS, HALF), BF16),
            pltpu.VMEM((ROWS, HALF), BF16),
            pltpu.VMEM((2, TOK, BLOCK), F32),
            pltpu.VMEM((2, TOK, BLOCK), BF16),
            pltpu.VMEM((2, TOK, BLOCK), BF16),
            pltpu.VMEM((TOK, BLOCK), BF16),
            pltpu.VMEM((TOK, BLOCK), BF16),
            pltpu.VMEM((3, 8, FF, BLOCK), BF16),
            dma((8,)), dma((8,)), dma((24,)), dma,
            dma((2, EXPERTS)), dma((2, EXPERTS)), dma((2,)), dma((2,)),
            dma((CHUNKS, 2, 2)), dma((CHUNKS, 2, 2)), dma((CHUNKS, 2)), dma((CHUNKS, 2)),
            dma((EXPERTS,)), dma((EXPERTS,)), dma((3,)), dma((3,)), dma((3, 8)),
        ],
        name="expert_backward",
        compiler_params=pltpu.CompilerParams(
            collective_id=0, has_side_effects=True, vmem_limit_bytes=56 * 2**20
        ),
    )(expert_ids.T, gate_weights.T, tokens_x, cotangent, w_gate[0], w_up[0], w_down[0])
    grad_gate, grad_up, grad_down = pl.pallas_call(
        finish,
        out_shape=(grad, grad, grad),
        in_specs=[anywhere] * 3,
        out_specs=[anywhere] * 3,
        scratch_shapes=[pltpu.VMEM((3, FF, D), BF16), dma((3, PIECES)), dma((3, PIECES))],
        name="finish",
        compiler_params=pltpu.CompilerParams(vmem_limit_bytes=56 * 2**20),
    )(*grads)
    return grad_tokens, grad_gate[None], grad_up[None], grad_down[None]


def solution(mesh):
    placed = (
        P("expert", None),
        P("expert", None),
        P("expert", None),
        P("expert", None),
        P("expert", "dp", None),
        P("expert", "dp", None),
        P("expert", "dp", None),
    )
    return jax.shard_map(
        local,
        mesh=mesh,
        in_specs=placed,
        out_specs=(
            P("expert", "dp"),
            P("expert", "dp", None),
            P("expert", "dp", None),
            P("expert", "dp", None),
        ),
        check_vma=False,
    )
```

```python
import functools

import jax
import jax.numpy as jnp
from jax import lax
from jax.experimental import pallas as pl
from jax.experimental.pallas import tpu as pltpu
from jax.sharding import PartitionSpec as P

MESH = pl.DeviceIdType.MESH
F32, BF16 = jnp.float32, jnp.bfloat16
D = 4096
HALF = 2048
QUARTER = 1024
BLOCK = 512
FF = 192
TOK = 128
CAP = 16
EXPERTS = 32
ROWS = EXPERTS * CAP
SIZES = (2, 2, 4, 4, 4, 4, 4, 4, 4)
CHUNKS = len(SIZES)
FIRST = tuple(sum(SIZES[:ch]) for ch in range(CHUNKS))

Z_C = ((1, 0), (-1, 0), (2, 0), (0, 1), (-1, 1), (1, 1), (-2, 1), (0, 0))
ON_CHIP = ((0, 0, 1), (0, 0, 0))
MESSAGES = tuple(
    (dy,) + Z_C[(k + 2 * n) % 8]
    for k in range(8)
    for n, dy in enumerate((1, 2, 3, 0))
    if (dy,) + Z_C[(k + 2 * n) % 8] not in ON_CHIP
) + ON_CHIP
CORE, SELF = EXPERTS - 2, EXPERTS - 1
REMOTE = tuple(range(SELF))


def nt(left, right):
    return lax.dot_general(left, right, (((1,), (1,)), ((), ())), preferred_element_type=F32)


def nn(left, right):
    return lax.dot_general(left, right, (((1,), (0,)), ((), ())), preferred_element_type=F32)


def tn(left, right):
    return lax.dot_general(left, right, (((0,), (0,)), ((), ())), preferred_element_type=F32)


def ranks(routes):
    ids0, ids1 = routes[0:1, :], routes[1:2, :]
    expert_row = lax.broadcasted_iota(jnp.int32, (EXPERTS, TOK), 0).astype(F32)
    earlier = (
        lax.broadcasted_iota(jnp.int32, (TOK, TOK), 0)
        < lax.broadcasted_iota(jnp.int32, (TOK, TOK), 1)
    )
    earlier = jnp.where(earlier, 1.0, 0.0).astype(BF16)
    hot0 = jnp.where(expert_row == ids0, 1.0, 0.0)
    hot1 = jnp.where(expert_row == ids1, 1.0, 0.0)
    before0 = nn(hot0.astype(BF16), earlier)
    before1 = nn(hot1.astype(BF16), earlier) + jnp.sum(hot0, axis=1, keepdims=True)
    return (
        jnp.sum(hot0 * before0, axis=0, keepdims=True),
        jnp.sum(hot1 * before1, axis=0, keepdims=True),
    )


def kernel(
    ids_ref, gate_ref, tok_hbm, cot_hbm, wg_hbm, wu_hbm, wd_hbm,
    gt_ref, gg_hbm, gu_hbm, gd_hbm,
    tok, tok_q, weights, onehot, gates, sent, sent_q, arrived, slope, swish, act, ggrad, ugrad,
    part_own, part_out, part_in, summed, returned, combined, fin_out, fin_in, fin_out2, fin_in2, grads,
    tok_sem, tok_q_sem, w_sem, self_sem,
    a_send, a_recv, k_send, k_recv, x_send, x_recv, p_send, p_recv, r_send, r_recv, s_send, s_recv, g_sem,
):
    dp, ex = lax.axis_index("dp"), lax.axis_index("expert")
    h, x = dp // 4, dp % 4
    y, l, c = ex // 8, (ex // 2) % 4, ex % 2
    z = h * 4 + l
    p = x % 2
    q = 1 - p
    turn = 1 - 2 * c

    def at(dx, dy, dz, dc):
        zz = (z + dz + 8) % 8
        return (
            (zz // 4) * 4 + (x + dx + 4) % 4,
            ((y + dy + 4) % 4) * 8 + (zz % 4) * 2 + (c + dc) % 2,
        )

    def remote(src, dst, send, recv, *offset):
        return pltpu.make_async_remote_copy(
            src, dst, send, recv, device_id=at(*offset), device_id_type=MESH
        )

    ins, q_ins, w_ins = [], [], []
    for i, src in enumerate((tok_hbm, cot_hbm)):
        for j in range(4):
            to = pl.ds(j * BLOCK, BLOCK)
            cols = pl.ds(pl.multiple_of((2 * j + p) * BLOCK, BLOCK), BLOCK)
            ins.append(pltpu.make_async_copy(src.at[:, cols], tok.at[i, :, to], tok_sem.at[4 * i + j]))
            cols = pl.ds(pl.multiple_of((2 * j + q) * BLOCK, BLOCK), BLOCK)
            q_ins.append(pltpu.make_async_copy(src.at[:, cols], tok_q.at[i, :, to], tok_q_sem.at[4 * i + j]))
    for i, src in enumerate((wg_hbm, wu_hbm, wd_hbm)):
        for b in range(8):
            to = pl.ds((b // 2) * BLOCK, BLOCK)
            w_ins.append(
                pltpu.make_async_copy(
                    src.at[:, pl.ds(b * BLOCK, BLOCK)], weights.at[i, b % 2, :, to], w_sem.at[8 * i + b]
                )
            )
    for copy in ins + q_ins + w_ins:
        copy.start()

    barrier = pltpu.get_barrier_semaphore()
    peers = [(0,) + MESSAGES[i] for i in REMOTE]
    peers += [(0, dy, -dz, dc) for dy, dz, dc in MESSAGES if abs(dz) == 2]
    peers += [(1, 0, 0, 0), (-1, 0, 0, 0), (2, 0, 0, 0), (0, 0, 4, 0)]
    for peer in peers:
        pl.semaphore_signal(barrier, inc=1, device_id=at(*peer), device_id_type=MESH)

    route = jnp.concatenate([ids_ref[...].astype(F32), gate_ref[...]], axis=0)
    rank0, rank1 = ranks(route)
    slot_row = lax.broadcasted_iota(jnp.int32, (CAP, TOK), 0).astype(F32)

    def slots(ch):
        for i in range(FIRST[ch], FIRST[ch] + SIZES[ch]):
            dy, dz, dc = MESSAGES[i]
            expert = ((y + turn * dy + 4) % 4) * 8 + ((l + turn * dz + 4) % 4) * 2 + (c + dc) % 2
            expert = expert.astype(F32)
            is0 = (slot_row == rank0) & (route[0:1, :] == expert)
            is1 = (slot_row == rank1) & (route[1:2, :] == expert)
            rows = pl.ds(i * CAP, CAP)
            onehot[rows, :] = jnp.where(is0 | is1, 1.0, 0.0)
            gate = jnp.where(is0, route[2:3, :], 0.0) + jnp.where(is1, route[3:4, :], 0.0)
            gates[rows, :] = jnp.broadcast_to(jnp.sum(gate, axis=1, keepdims=True), (CAP, TOK))

    def chunk_rows(ch, less=0):
        return pl.ds(FIRST[ch] * CAP, SIZES[ch] * CAP - less)

    def out_copy(i, kind):
        dy, dz, dc = MESSAGES[i]
        rows = pl.ds(i * CAP, CAP)
        return remote(
            sent.at[kind, rows], arrived.at[p, kind, rows], a_send.at[kind, i], a_recv.at[kind, i], 0, turn * dy, turn * dz, dc
        )

    def core_copy(kind):
        return remote(
            sent_q.at[kind], arrived.at[q, kind, pl.ds(CORE * CAP, CAP)], k_send.at[kind], k_recv.at[kind], 0, 0, 0, 1
        )

    def send_slots(ch, kind):
        rows = chunk_rows(ch)
        picked = nn(onehot[rows, :].astype(BF16), tok[kind])
        if kind == 1:
            picked = picked * gates[rows, 0:1]
        picked = picked.astype(BF16)
        sent[kind, rows, :] = picked
        for i in range(FIRST[ch], FIRST[ch] + SIZES[ch]):
            if i == SELF:
                arrived[p, kind, pl.ds(SELF * CAP, CAP), :] = picked[(SELF - FIRST[ch]) * CAP :]
            else:
                out_copy(i, kind).start()

    def send_local(kind):
        rows = pl.ds(CORE * CAP, 2 * CAP)
        picked = nn(onehot[rows, :].astype(BF16), tok_q[kind])
        if kind == 1:
            picked = picked * gates[rows, 0:1]
        picked = picked.astype(BF16)
        sent_q[kind] = picked[0:CAP]
        core_copy(kind).start()
        arrived[q, kind, pl.ds(SELF * CAP, CAP), :] = picked[CAP:]

    def sides(rows, src, dst, send, recv):
        return [
            remote(src(rows, cols), dst(rows, cols), send(side), recv(side), dx, 0, 0, 0)
            for side, dx, cols in ((0, 1, pl.ds(0, QUARTER)), (1, -1, pl.ds(QUARTER, QUARTER)))
        ]

    def spread(ch, kind, half):
        ref = lambda rows, cols: arrived.at[half, kind, rows, cols]
        rows = chunk_rows(ch, 2 * CAP if ch == CHUNKS - 1 else 0)
        return sides(
            rows, ref, ref, lambda side: x_send.at[ch, kind, side], lambda side: x_recv.at[ch, kind, side]
        )

    def forward(ch, kind):
        for i in range(FIRST[ch], FIRST[ch] + SIZES[ch]):
            if i not in (CORE, SELF):
                out_copy(i, kind).wait_recv()
        for copy in spread(ch, kind, p):
            copy.start()

    def parts(ch):
        return sides(
            chunk_rows(ch), lambda rows, cols: part_out.at[rows, cols], lambda rows, cols: part_in.at[rows, cols],
            lambda side: p_send.at[ch, side], lambda side: p_recv.at[ch, side],
        )

    def wait_rows(ch, kind):
        for copy in spread(ch, kind, q):
            copy.wait_recv()
        if ch == CHUNKS - 1:
            out_copy(CORE, kind).wait_recv()
            core_copy(kind).wait_recv()

    def compute_tokens(ch):
        wait_rows(ch, 0)
        rows = chunk_rows(ch)
        gate_pre = nt(arrived[0, 0, rows, :], weights[0, 0]) + nt(arrived[1, 0, rows, :], weights[0, 1])
        up_pre = nt(arrived[0, 0, rows, :], weights[1, 0]) + nt(arrived[1, 0, rows, :], weights[1, 1])
        s = jax.nn.sigmoid(gate_pre)
        value = gate_pre * s
        act[rows, :] = (value * up_pre).astype(BF16)
        swish[rows, :] = value
        slope[rows, :] = up_pre * (s * (1.0 + gate_pre * (1.0 - s)))

    def compute_cotangents(ch):
        wait_rows(ch, 1)
        rows = chunk_rows(ch)
        act_grad = nt(arrived[0, 1, rows, :], weights[2, 0]) + nt(arrived[1, 1, rows, :], weights[2, 1])
        gate_grad = (act_grad * slope[rows, :]).astype(BF16)
        up_grad = (act_grad * swish[rows, :]).astype(BF16)
        ggrad[rows, :] = gate_grad
        ugrad[rows, :] = up_grad
        part_out[rows, :] = (nn(gate_grad, weights[0, q]) + nn(up_grad, weights[1, q])).astype(BF16)
        for copy in parts(ch):
            copy.start()
        part_own[rows, :] = nn(gate_grad, weights[0, p]) + nn(up_grad, weights[1, p])

    def back(i):
        dy, dz, dc = MESSAGES[i]
        rows, sign = pl.ds(i * CAP, CAP), turn if dc else -turn
        return remote(summed.at[rows], returned.at[rows], r_send.at[i], r_recv.at[i], 0, sign * dy, sign * dz, dc)

    own_rows = pl.ds(SELF * CAP, CAP)
    self_back = pltpu.make_async_copy(summed.at[own_rows], returned.at[own_rows], self_sem)

    def give_back(ch):
        for copy in parts(ch):
            copy.wait_recv()
        rows = chunk_rows(ch)
        summed[rows, :] = (part_own[rows, :] + part_in[rows, :].astype(F32)).astype(BF16)
        for i in range(FIRST[ch], FIRST[ch] + SIZES[ch]):
            if i == SELF:
                self_back.start()
            else:
                back(i).start()

    slots(0)
    for copy in ins:
        copy.wait()
    pl.semaphore_wait(barrier, len(peers))
    for ch in range(CHUNKS):
        if ch:
            slots(ch)
        send_slots(ch, 0)
        send_slots(ch, 1)
    for copy in q_ins:
        copy.wait()
    send_local(0)
    send_local(1)
    pick = onehot[...].T.astype(BF16)
    forward(0, 0)
    forward(0, 1)
    for copy in w_ins:
        copy.wait()
    for ch in range(CHUNKS):
        if ch + 1 < CHUNKS:
            forward(ch + 1, 0)
        compute_tokens(ch)
        if ch + 1 < CHUNKS:
            forward(ch + 1, 1)
        compute_cotangents(ch)
        if ch:
            give_back(ch - 1)
    give_back(CHUNKS - 1)

    outs = (gg_hbm, gu_hbm, gd_hbm)

    def grad_copy(i, b):
        return pltpu.make_async_copy(
            grads.at[i, b], outs[i].at[:, pl.ds(pl.multiple_of(b * BLOCK, BLOCK), BLOCK)], g_sem.at[i, b]
        )

    @pl.loop(0, 8)
    def _(b):
        half, cols = b % 2, pl.ds(pl.multiple_of((b // 2) * BLOCK, BLOCK), BLOCK)
        inputs = arrived[half, 0, :, cols]
        grads[0, b] = tn(ggrad[...], inputs).astype(BF16)
        grad_copy(0, b).start()
        grads[1, b] = tn(ugrad[...], inputs).astype(BF16)
        grad_copy(1, b).start()
        grads[2, b] = tn(act[...], arrived[half, 1, :, cols]).astype(BF16)
        grad_copy(2, b).start()

    self_back.wait()
    for i in REMOTE:
        back(i).wait_recv()

    j_x, j_z = x // 2, h

    def fin_x(k):
        return remote(fin_out.at[k], fin_in.at[k], s_send.at[k], s_recv.at[k], 2, 0, 0, 0)

    fin_z = remote(fin_out2, fin_in2, s_send.at[2], s_recv.at[2], 0, 0, 4, 0)

    def token_block(b_z, b_x):
        cols = pl.ds(pl.multiple_of((2 * b_z + b_x) * BLOCK, BLOCK), BLOCK)
        return nn(pick, returned[:, cols])

    for k, b_z in enumerate((1 - j_z, j_z)):
        fin_out[k] = token_block(b_z, 1 - j_x).astype(BF16)
        fin_x(k).start()
    for k, b_z in enumerate((1 - j_z, j_z)):
        combined[k] = token_block(b_z, j_x)
    fin_x(0).wait_recv()
    fin_out2[...] = (combined[0] + fin_in[0].astype(F32)).astype(BF16)
    fin_z.start()
    fin_x(1).wait_recv()
    total = combined[1] + fin_in[1].astype(F32)
    fin_z.wait_recv()
    gt_ref[...] = (total + fin_in2[...].astype(F32)).astype(BF16)

    for i in REMOTE:
        out_copy(i, 0).wait_send()
        out_copy(i, 1).wait_send()
        back(i).wait_send()
    for kind in range(2):
        core_copy(kind).wait_send()
    for ch in range(CHUNKS):
        for copy in spread(ch, 0, p) + spread(ch, 1, p) + parts(ch):
            copy.wait_send()
    for copy in (fin_x(0), fin_x(1), fin_z):
        copy.wait_send()

    @pl.loop(0, 8)
    def _(b):
        for i in range(3):
            grad_copy(i, b).wait()


PIECES = 2


def finish(*refs):
    ins, outs, held, in_sem, out_sem = refs[:3], refs[3:6], refs[6], refs[7], refs[8]
    copies = []
    for i in range(3):
        for k in range(PIECES):
            rows = pl.ds(k * (FF // PIECES), FF // PIECES)
            copies.append((
                pltpu.make_async_copy(ins[i].at[rows], held.at[i, rows], in_sem.at[i, k]),
                pltpu.make_async_copy(held.at[i, rows], outs[i].at[rows], out_sem.at[i, k]),
            ))
    for copy, _ in copies:
        copy.start()
    for copy, on in copies:
        copy.wait()
        on.start()
    for _, on in copies:
        on.wait()


def local(tokens_x, cotangent, expert_ids, gate_weights, w_gate, w_up, w_down):
    vmem = pl.BlockSpec(memory_space=pltpu.VMEM)
    anywhere = pl.BlockSpec(memory_space=pl.ANY)
    dma = pltpu.SemaphoreType.DMA
    grad = jax.ShapeDtypeStruct((FF, D), BF16)
    grad_tokens, *grads = pl.pallas_call(
        kernel,
        out_shape=(jax.ShapeDtypeStruct((TOK, BLOCK), BF16), grad, grad, grad),
        in_specs=[vmem] * 2 + [anywhere] * 5,
        out_specs=(vmem, anywhere, anywhere, anywhere),
        scratch_shapes=[
            pltpu.VMEM((2, TOK, HALF), BF16),
            pltpu.VMEM((2, TOK, HALF), BF16),
            pltpu.VMEM((3, 2, FF, HALF), BF16),
            pltpu.VMEM((ROWS, TOK), F32),
            pltpu.VMEM((ROWS, TOK), F32),
            pltpu.VMEM((2, ROWS, HALF), BF16),
            pltpu.VMEM((2, CAP, HALF), BF16),
            pltpu.VMEM((2, 2, ROWS, HALF), BF16),
            pltpu.VMEM((ROWS, FF), F32),
            pltpu.VMEM((ROWS, FF), F32),
            pltpu.VMEM((ROWS, FF), BF16),
            pltpu.VMEM((ROWS, FF), BF16),
            pltpu.VMEM((ROWS, FF), BF16),
            pltpu.VMEM((ROWS, HALF), F32),
            pltpu.VMEM((ROWS, HALF), BF16),
            pltpu.VMEM((ROWS, HALF), BF16),
            pltpu.VMEM((ROWS, HALF), BF16),
            pltpu.VMEM((ROWS, HALF), BF16),
            pltpu.VMEM((2, TOK, BLOCK), F32),
            pltpu.VMEM((2, TOK, BLOCK), BF16),
            pltpu.VMEM((2, TOK, BLOCK), BF16),
            pltpu.VMEM((TOK, BLOCK), BF16),
            pltpu.VMEM((TOK, BLOCK), BF16),
            pltpu.VMEM((3, 8, FF, BLOCK), BF16),
            dma((8,)), dma((8,)), dma((24,)), dma,
            dma((2, EXPERTS)), dma((2, EXPERTS)), dma((2,)), dma((2,)),
            dma((CHUNKS, 2, 2)), dma((CHUNKS, 2, 2)), dma((CHUNKS, 2)), dma((CHUNKS, 2)),
            dma((EXPERTS,)), dma((EXPERTS,)), dma((3,)), dma((3,)), dma((3, 8)),
        ],
        name="expert_backward",
        compiler_params=pltpu.CompilerParams(
            collective_id=0, has_side_effects=True, vmem_limit_bytes=56 * 2**20
        ),
    )(expert_ids.T, gate_weights.T, tokens_x, cotangent, w_gate[0], w_up[0], w_down[0])
    grad_gate, grad_up, grad_down = pl.pallas_call(
        finish,
        out_shape=(grad, grad, grad),
        in_specs=[anywhere] * 3,
        out_specs=[anywhere] * 3,
        scratch_shapes=[pltpu.VMEM((3, FF, D), BF16), dma((3, PIECES)), dma((3, PIECES))],
        name="finish",
        compiler_params=pltpu.CompilerParams(vmem_limit_bytes=56 * 2**20),
    )(*grads)
    return grad_tokens, grad_gate[None], grad_up[None], grad_down[None]


def solution(mesh):
    placed = (
        P("expert", None),
        P("expert", None),
        P("expert", None),
        P("expert", None),
        P("expert", "dp", None),
        P("expert", "dp", None),
        P("expert", "dp", None),
    )
    return jax.shard_map(
        local,
        mesh=mesh,
        in_specs=placed,
        out_specs=(
            P("expert", "dp"),
            P("expert", "dp", None),
            P("expert", "dp", None),
            P("expert", "dp", None),
        ),
        check_vma=False,
    )
```
